32 devices in a mesh: grp: 2 (over y), row: 4 (over z), rhs: 2 (over x), sub: 2 (over core).
Axes of the slice: x: 2, y: 2, z: 4, core: 2. Of those that a mesh axis runs over, the one named last changes fastest.
Arguments:
- right_sides: float32 [8, 512, 256], P('grp', ('row', 'sub'), 'rhs'), parts along dimension 0, may hold values from -6 to 6
- diag_inverse: float32 [8, 512, 512], P('grp', ('row', 'sub')), parts along dimension 0, may hold values from -1 to 3, as said below
- factor_below: float32 [6, 512, 256], P('grp', ('row', 'sub')), parts along dimension 0, may hold values from -0.375 to 0.375
- block_lists: int32 [6, 4, 2], P('grp', 'row'), parts along dimension 0, may hold values from 0 to 11, as said below
Outputs:
- solution: float32 [8, 512, 256], P('grp', ('row', 'sub'), 'rhs'), parts along dimension 0
The draws below stay inside these ranges and needn't reach their ends.
There are 2 independent parts, one for each index of `grp`. The reference program is written for one: setup_inputs(seed, part) draws one part's arguments, and reference() takes and returns one part's arrays. A program takes and returns all parts, laid end to end along the dimension named above; each array names one. Nothing has to cross between parts.
Inputs may be any that keep to these rules, and one draw needn't show every extreme that they name: `diag_inverse`: upper triangular with diagonal entries between 0.5 and 3. block_lists[t - 1, i, :] names 2 different blocks of supernodes 0 to t - 1; entry 0 is block i of supernode t - 1.
All inputs are finite; a program needn't handle non-finite values.
Results may differ from the reference program's by a relative error of at most 0.00017.
Values sent between devices are 32-bit elements; how exact they have to be, the bound alone decides.
No kernel may reach another device: no remote copies, remote signals or barrier semaphores. Data moves between devices by JAX's collectives and lax.ppermute only.
A program may use at most 64 MiB of HBM per device.

```python
import math
import jax
import jax.numpy as jnp
from jax import lax

S = 4
BS = 128
NB = 4
NS = 512
NNZ = 2
R = 256


def draw_diag_inverse(key, part):
    first_key, second_key = jax.random.split(key)
    row_ids = jnp.arange(NS)[:, None]
    col_ids = jnp.arange(NS)[None, :]
    below_part = jax.random.normal(first_key, (S, NS, NS), jnp.float32)
    diagonal = jax.random.uniform(second_key, (S, NS, 1), jnp.float32, 1.0, 2.0)
    spread = 1.2 / math.sqrt(NS)
    return jnp.where(row_ids < col_ids, below_part * spread, 0.0) + jnp.where(row_ids == col_ids, diagonal, 0.0)


def draw_block_lists(key, part):
    per_super = []
    for t in range(1, S):
        count_prior = t * NB

        def for_row(i):
            row_key = jax.random.fold_in(jax.random.fold_in(key, t), i)
            forced = (t - 1) * NB + i
            others = jax.random.permutation(row_key, count_prior - 1)[:NNZ - 1].astype(jnp.int32)
            others = others + (others >= forced).astype(jnp.int32)
            return jnp.concatenate([jnp.full((1,), forced, jnp.int32), others])
        per_super.append(jax.vmap(for_row)(jnp.arange(NB, dtype=jnp.int32)))
    return jnp.stack(per_super).astype(jnp.int32)


def block_scale(own_key, extent, cuts, least, high):
    factor_of = 1.0
    for position, blocks in cuts:
        draws = jax.random.uniform(jax.random.fold_in(jax.random.fold_in(own_key, 6), position), (blocks,), jnp.float32, least / len(cuts), high / len(cuts))
        factor_of = factor_of * jnp.repeat(jnp.exp(draws), extent[position] // blocks).reshape((-1,) + (1,) * (len(extent) - 1 - position))
    return factor_of


def gaussian(own_key, extent, width, reach, cuts=(), kind=jnp.bfloat16):
    factor_of = block_scale(own_key, extent, cuts, -0.22, 0.18) if cuts else 1.0
    result = jax.random.normal(own_key, extent, jnp.float32) * width * factor_of
    return jnp.minimum(jnp.maximum(result, -reach), reach).astype(kind)


def setup_inputs(seed: int = 0, part: int = 0) -> dict:
    splits = jax.random.split(jax.random.key(seed), 5)
    part_splits = jax.random.split(jax.random.fold_in(splits[4], part), 5)
    return {
        "right_sides": gaussian(part_splits[0], (S, NS, R), 1.0, 6.0, ((1, 8), (2, 2)), jnp.float32),
        "diag_inverse": draw_diag_inverse(jax.random.fold_in(jax.random.fold_in(splits[4], part), 71), part),
        "factor_below": gaussian(part_splits[2], (S - 1, NS, NNZ * BS), (NNZ * BS) ** -0.5, 0.375, ((1, 8),), jnp.float32),
        "block_lists": draw_block_lists(jax.random.fold_in(jax.random.fold_in(splits[4], part), 71), part),
    }


def reference(right_sides, diag_inverse, factor_below, block_lists):
    highest = lax.Precision.HIGHEST
    blocks = jnp.zeros((S * NB, BS, R), jnp.float32)
    results = []
    for t in range(S):
        residual = right_sides[t]
        if t > 0:
            picked = blocks[block_lists[t - 1]].reshape(NB, NNZ * BS, R)
            factor = factor_below[t - 1].reshape(NB, BS, NNZ * BS)
            update = jnp.einsum("ibk,ikr->ibr", factor, picked, precision=highest).reshape(NS, R)
            residual = residual - update
        solved_now = jnp.dot(diag_inverse[t].T, residual, precision=highest, preferred_element_type=jnp.float32)
        blocks = blocks.at[t * NB:(t + 1) * NB].set(solved_now.reshape(NB, BS, R))
        results.append(solved_now)
    return jnp.stack(results)
```

```python
import functools

import jax
import jax.numpy as jnp
from jax import lax
from jax.experimental import pallas as pl
from jax.experimental.pallas import tpu as pltpu
from jax.sharding import PartitionSpec as P

S = 4
BS = 128
LANES = 128
VMEM = pl.BlockSpec(memory_space=pltpu.VMEM)
SMEM = pl.BlockSpec(memory_space=pltpu.SMEM)


def split(a):
    high = a.astype(jnp.bfloat16)
    return high, (a - high.astype(jnp.float32)).astype(jnp.bfloat16)


def dot(a, b):
    return jnp.dot(a, b, preferred_element_type=jnp.float32)


def product(a, b_high, b_low):
    a_high, a_low = split(a)
    rows = a.shape[0]
    both = dot(jnp.concatenate([a_high, a_low], axis=0), b_high)
    return both[:rows] + both[rows:] + dot(a_high, b_low)


def call(kernel, outs, scratch=()):
    return functools.partial(
        pl.pallas_call,
        kernel,
        out_shape=outs,
        scratch_shapes=list(scratch),
        compiler_params=pltpu.CompilerParams(vmem_limit_bytes=40 * 1024 * 1024),
    )


def first_kernel(quarter, ids, own, other, keep, send, turned, terms):
    width = own.shape[1] - LANES
    blocks = width // BS
    turned[...] = jnp.concatenate([own[:, width:], other[:, width:]], axis=0).T
    sides = turned[pl.ds(pl.multiple_of(ids[0] * 2 * quarter, 2 * quarter), 2 * quarter), :]
    high, low = split(jnp.concatenate([own[:, :width], other[:, :width]], axis=0))
    share = product(sides, high, low)
    for i in range(blocks):
        terms[i] = share[:, i * BS : (i + 1) * BS]
    keep[...] = terms[:, pl.ds(pl.multiple_of(ids[1] * quarter, quarter), quarter), :]
    send[...] = terms[:, pl.ds(pl.multiple_of((1 - ids[1]) * quarter, quarter), quarter), :]


def prepare_kernel(quarter, ids, a0, a1, a2, a3, diag_high, diag_low, below_high, below_low, sides, turned):
    width = diag_high.shape[1]
    depth = below_high.shape[1]
    first = pl.multiple_of(ids[0] * 2 * quarter + ids[1] * quarter, quarter)
    for j, (one, two) in enumerate(((a0, a1), (a2, a3))):
        high, low = split(jnp.concatenate([one[:, :width], two[:, :width]], axis=0))
        diag_high[j * BS : (j + 1) * BS, :] = high
        diag_low[j * BS : (j + 1) * BS, :] = low
        below = jnp.concatenate([one[:, width : width + depth], two[:, width : width + depth]], axis=0)
        high, low = split(below.T)
        below_high[j] = high
        below_low[j] = low
        turned[...] = jnp.concatenate([one[:, width + depth :], two[:, width + depth :]], axis=0).T
        sides[j] = turned[pl.ds(first, quarter), :]


def step_kernel(listed, lists, *refs):
    stored = refs[:-9]
    keep, recv, diag_high, diag_low, below_high, below_low, sides, solved, share = refs[-9:]
    blocks = keep.shape[0]
    before = solved.shape[0] - blocks
    if before:
        solved[:before] = stored[0][...]
    solved[before:] = keep[...] + recv[...]
    residuals = []
    for j in range(2):
        picked = jnp.concatenate([solved[lists[j * listed + k]] for k in range(listed)], axis=1)
        residuals.append(sides[j] - product(picked, below_high[j], below_low[j]))
    result = product(jnp.concatenate(residuals, axis=1), diag_high[...], diag_low[...])
    for i in range(blocks):
        share[i] = result[:, i * BS : (i + 1) * BS]


def last_kernel(ids, stored, keep, recv, own, send):
    blocks = keep.shape[0]
    for t in range(S - 1):
        own[t] = stored[t * blocks + ids[2]]
        send[t] = stored[t * blocks + ids[3]]
    own[S - 1] = keep[ids[2]] + recv[ids[2]]
    send[S - 1] = keep[ids[3]] + recv[ids[3]]


def place_kernel(quarter, ids, a0, a1, a2, a3, out, whole):
    core, half = ids[0], ids[1]
    rows = out.shape[1]
    for t in range(S):
        for a, c, h in ((a0, core, half), (a1, core, 1 - half), (a2, 1 - core, half), (a3, 1 - core, 1 - half)):
            whole[pl.ds(pl.multiple_of((2 * c + h) * quarter, quarter), quarter), :] = a[t]
        turned = whole[...].T
        out[t] = jnp.where(core == 0, turned[:rows], turned[rows:])


def body(count, right_sides, diag_inverse, factor_below, block_lists):
    half_count = count // 2
    quarter = right_sides.shape[2] // 4
    blocks = diag_inverse.shape[2] // BS
    width = diag_inverse.shape[2]
    depth = factor_below.shape[2]
    listed = block_lists.shape[2]
    row, core = lax.axis_index("row"), lax.axis_index("sub")
    half = row // half_count
    team = lax.rem(row + half_count, count)
    ids = jnp.stack([core, half, row, team]).astype(jnp.int32)

    def to_core(a):
        return lax.ppermute(a, "sub", [(0, 1), (1, 0)])

    def to_row(a, bit):
        return lax.ppermute(a, "row", [(i, i ^ bit) for i in range(count)])

    f32, bf16 = jnp.float32, jnp.bfloat16
    shape = jax.ShapeDtypeStruct
    piece = shape((blocks, quarter, BS), f32)

    first = jnp.concatenate([diag_inverse[0], right_sides[0]], axis=1)
    keep, send = call(
        functools.partial(first_kernel, quarter),
        (piece, piece),
        [pltpu.VMEM((4 * quarter, BS), f32), pltpu.VMEM((blocks, 2 * quarter, BS), f32)],
    )(in_specs=[SMEM, VMEM, VMEM])(ids, first, to_core(first))

    lists = jnp.concatenate([block_lists[:, 0], to_row(block_lists[:, 0], half_count)], axis=1)
    rest = [
        jnp.concatenate([diag_inverse[t], factor_below[t - 1], right_sides[t]], axis=1) for t in range(1, S)
    ]
    prepared = []
    for own in rest:
        other = to_row(own, half_count)
        prepared.append(
            call(
                functools.partial(prepare_kernel, quarter),
                (
                    shape((2 * BS, width), bf16),
                    shape((2 * BS, width), bf16),
                    shape((2, depth, BS), bf16),
                    shape((2, depth, BS), bf16),
                    shape((2, quarter, BS), f32),
                ),
                [pltpu.VMEM((4 * quarter, BS), f32)],
            )(in_specs=[SMEM] + [VMEM] * 4)(ids, own, to_core(own), other, to_core(other))
        )

    def shares(a):
        bit = half_count // 2
        while bit > 1:
            a = a + to_row(a, bit)
            bit //= 2
        return a, to_row(a, 1)

    keep, recv = shares(keep + to_row(send, half_count))
    stored = ()
    for t in range(1, S):
        solved, share = call(
            functools.partial(step_kernel, listed),
            (shape((t * blocks, quarter, BS), f32), piece),
        )(in_specs=[SMEM] + [VMEM] * (len(stored) + 7))(
            lists[t - 1], *stored, keep, recv, *prepared[t - 1]
        )
        stored = (solved,)
        keep, recv = shares(share)
    block = shape((S, quarter, BS), f32)
    own, send = call(last_kernel, (block, block))(in_specs=[SMEM] + [VMEM] * 3)(ids, *stored, keep, recv)
    other = to_row(send, half_count)
    return call(
        functools.partial(place_kernel, quarter),
        shape((S, BS // 2, 4 * quarter), f32),
        [pltpu.VMEM((4 * quarter, BS), f32)],
    )(in_specs=[SMEM] + [VMEM] * 4)(ids, own, other, to_core(own), to_core(other))


def solution(mesh):
    in_specs = (
        P("grp", ("row", "sub"), "rhs"),
        P("grp", ("row", "sub"), None),
        P("grp", ("row", "sub"), None),
        P("grp", "row", None),
    )
    out_specs = P("grp", ("row", "sub"), "rhs")
    step = functools.partial(body, mesh.shape["row"])
    return jax.shard_map(step, mesh=mesh, in_specs=in_specs, out_specs=out_specs, check_vma=False)
```

```python
import functools

import jax
import jax.numpy as jnp
from jax import lax
from jax.experimental import pallas as pl
from jax.experimental.pallas import tpu as pltpu
from jax.sharding import PartitionSpec as P

K = {'first': 0.3, 'prep': [1, 16, 16], 'step': [4, 1, 0.3], 'bulk': ['send', 'share0', 'recv0'], 'swap': ['recv0', 'recv0', 'recv1']}
S = 4
BS = 128
LANES = 128
VMEM = pl.BlockSpec(memory_space=pltpu.VMEM)
SMEM = pl.BlockSpec(memory_space=pltpu.SMEM)


def split(a):
    high = a.astype(jnp.bfloat16)
    return high, (a - high.astype(jnp.float32)).astype(jnp.bfloat16)


def dot(a, b):
    return jnp.dot(a, b, preferred_element_type=jnp.float32)


def product(a, b_high, b_low):
    a_high, a_low = split(a)
    rows = a.shape[0]
    both = dot(jnp.concatenate([a_high, a_low], axis=0), b_high)
    return both[:rows] + both[rows:] + dot(a_high, b_low)


def call(kernel, outs, scratch=(), cost=0):
    return functools.partial(
        pl.pallas_call,
        kernel,
        out_shape=outs,
        scratch_shapes=list(scratch),
        compiler_params=pltpu.CompilerParams(vmem_limit_bytes=40 * 1024 * 1024),
        cost_estimate=pl.CostEstimate(flops=int(cost * 1e9), bytes_accessed=1000, transcendentals=0),
    )


def first_kernel(quarter, ids, lists, own, other, keep, send, turned, terms):
    width = own.shape[1] - LANES
    blocks = width // BS
    turned[...] = jnp.concatenate([own[:, width:], other[:, width:]], axis=0).T
    sides = turned[pl.ds(pl.multiple_of(ids[0] * 2 * quarter, 2 * quarter), 2 * quarter), :]
    high, low = split(jnp.concatenate([own[:, :width], other[:, :width]], axis=0))
    share = product(sides, high, low)
    for i in range(blocks):
        terms[i] = share[:, i * BS : (i + 1) * BS]
    keep[...] = terms[:, pl.ds(pl.multiple_of(ids[1] * quarter, quarter), quarter), :]
    send[:blocks] = terms[:, pl.ds(pl.multiple_of((1 - ids[1]) * quarter, quarter), quarter), :]
    lane = lax.broadcasted_iota(jnp.int32, (quarter, BS), 1)
    told = jnp.zeros((quarter, BS), jnp.float32)
    for i in range(lists.shape[0]):
        for k in range(lists.shape[1]):
            told = jnp.where(lane == i * lists.shape[1] + k, lists[i, k].astype(jnp.float32), told)
    send[blocks] = told


def prepare_kernel(quarter, ids, a0, a1, a2, a3, diag_high, diag_low, below_high, below_low, sides, turned):
    width = diag_high.shape[1]
    depth = below_high.shape[1]
    first = pl.multiple_of(ids[0] * 2 * quarter + ids[1] * quarter, quarter)
    for j, (one, two) in enumerate(((a0, a1), (a2, a3))):
        high, low = split(jnp.concatenate([one[:, :width], two[:, :width]], axis=0))
        diag_high[j * BS : (j + 1) * BS, :] = high
        diag_low[j * BS : (j + 1) * BS, :] = low
        below = jnp.concatenate([one[:, width : width + depth], two[:, width : width + depth]], axis=0)
        high, low = split(below.T)
        below_high[j] = high
        below_low[j] = low
        turned[...] = jnp.concatenate([one[:, width + depth :], two[:, width + depth :]], axis=0).T
        sides[j] = turned[pl.ds(first, quarter), :]


def advance(listed, lists, stored, refs, solved):
    keep, recv, diag_high, diag_low, below_high, below_low, sides = refs
    before = solved.shape[0] - keep.shape[0]
    if before:
        solved[:before] = stored[0][...]
    solved[before:] = keep[...] + recv[...]
    residuals = []
    for j in range(2):
        picked = jnp.concatenate([solved[lists[j, k]] for k in range(listed)], axis=1)
        residuals.append(sides[j] - product(picked, below_high[j], below_low[j]))
    return product(jnp.concatenate(residuals, axis=1), diag_high[...], diag_low[...])


def step_kernel(listed, lists, *refs):
    solved, share = refs[-2:]
    result = advance(listed, lists, refs[:-9], refs[-9:-2], solved)
    for i in range(share.shape[0]):
        share[i] = result[:, i * BS : (i + 1) * BS]


def give(ids, solved, share, own, near, far, both):
    blocks = share.shape[0]
    for t in range(S - 1):
        own[t] = solved[t * blocks + ids[2]]
        near[t] = solved[t * blocks + ids[3]]
    own[S - 1] = share[ids[2]]
    near[S - 1] = share[ids[3]]
    far[...] = share[ids[4]]
    both[...] = share[ids[5]]


def last_kernel(listed, ids, lists, *refs):
    own, near, far, both, solved, share = refs[-6:]
    result = advance(listed, lists, refs[:-13], refs[-13:-6], solved)
    for i in range(share.shape[0]):
        share[i] = result[:, i * BS : (i + 1) * BS]
    give(ids, solved, share, own, near, far, both)


def place_kernel(quarter, ids, *refs):
    quarters, out, whole = refs[:-2], refs[-2], refs[-1]
    core, half = ids[0], ids[1]
    rows = out.shape[1]
    places = ((core, half), (core, 1 - half), (1 - core, half), (1 - core, 1 - half))
    for t in range(S):
        for i, (c, h) in enumerate(places):
            part = quarters[2 * i][t]
            if t == S - 1:
                part = part + quarters[2 * i + 1][...]
            whole[pl.ds(pl.multiple_of((2 * c + h) * quarter, quarter), quarter), :] = part
        mine = jnp.where(core == 0, whole[:, :rows], whole[:, rows:])
        out[t] = mine.T


def body(count, right_sides, diag_inverse, factor_below, block_lists):
    quarter = right_sides.shape[2] // 4
    blocks = diag_inverse.shape[2] // BS
    width = diag_inverse.shape[2]
    depth = factor_below.shape[2]
    listed = block_lists.shape[2]
    top = count // 2
    row, core = lax.axis_index("row"), lax.axis_index("sub")
    half = lax.rem(row, 2)
    team = row + 1 - 2 * half
    far = lax.rem(row + top, count)
    ids = jnp.stack([core, half, row, team, far, far + 1 - 2 * half]).astype(jnp.int32)

    def to_core(a):
        return lax.ppermute(a, "sub", [(0, 1), (1, 0)])

    def to_row(a, bit):
        return lax.ppermute(a, "row", [(i, i ^ bit) for i in range(count)])

    def after(a, *others):
        return lax.optimization_barrier((a, *others))[0]

    f32, bf16 = jnp.float32, jnp.bfloat16
    shape = jax.ShapeDtypeStruct
    piece = shape((blocks, quarter, BS), f32)

    def total(a):
        bit = 2
        while bit < top:
            a = a + to_row(a, bit)
            bit *= 2
        return a, to_row(a, top)

    def prepare(t, own, own_core, other, other_core):
        return call(
            functools.partial(prepare_kernel, quarter),
            (
                shape((2 * BS, width), bf16),
                shape((2 * BS, width), bf16),
                shape((2, depth, BS), bf16),
                shape((2, depth, BS), bf16),
                shape((2, quarter, BS), f32),
            ),
            [pltpu.VMEM((4 * quarter, BS), f32)],
            K["prep"][t - 1],
        )(in_specs=[SMEM] + [VMEM] * 4)(ids, own, own_core, other, other_core)

    first = jnp.concatenate([diag_inverse[0], right_sides[0]], axis=1)
    first_core = to_core(first)
    keep, send = call(
        functools.partial(first_kernel, quarter),
        (piece, shape((blocks + 1, quarter, BS), f32)),
        [pltpu.VMEM((4 * quarter, BS), f32), pltpu.VMEM((blocks, 2 * quarter, BS), f32)],
        K["first"],
    )(in_specs=[SMEM, SMEM, VMEM, VMEM])(ids, block_lists[:, 0], first, first_core)
    got = to_row(send, 1)

    diag, below, sides, _ = lax.optimization_barrier((diag_inverse, factor_below, right_sides, send))
    rest = [jnp.concatenate([diag[t], below[t - 1], sides[t]], axis=1) for t in range(1, S)]
    rest_core = [to_core(a) for a in rest]

    share = keep + got[:blocks]
    told = got[blocks, 0, : (S - 1) * listed].reshape(S - 1, listed).astype(jnp.int32)
    lists = jnp.stack([block_lists[:, 0], told], axis=1)

    gates = {"send": send, "share0": share, "core1": rest_core[0], "core2": rest_core[1], "core3": rest_core[2]}
    stored = ()
    others = {}

    def bulk(u):
        if u not in others and K["bulk"][u - 1] in gates:
            others[u] = to_row(after(rest[u - 1], gates[K["bulk"][u - 1]]), 1)

    for t in range(1, S):
        for u in range(1, S):
            bulk(u)
        keep, recv = total(share)
        gates[f"recv{t - 1}"] = recv
        for u in range(1, S):
            bulk(u)
        other = others[t]
        g = K["swap"][t - 1]
        other_core = to_core(after(other, gates[g]) if g else other)
        gates[f"other{t}"] = other_core
        for u in range(1, S):
            bulk(u)
        operands = (*stored, keep, recv, *prepare(t, rest[t - 1], rest_core[t - 1], other, other_core))
        gates[f"prep{t}"] = operands[-1]
        for u in range(1, S):
            bulk(u)
        solved_shape = shape((t * blocks, quarter, BS), f32)
        if t < S - 1 or top > 2:
            solved, share = call(functools.partial(step_kernel, listed), (solved_shape, piece), (), K["step"][t - 1])(
                in_specs=[SMEM] + [VMEM] * len(operands)
            )(lists[t - 1], *operands)
            stored = (solved,)
            gates[f"share{t}"] = share

    block = shape((quarter, BS), f32)
    kept = shape((S, quarter, BS), f32)
    gifts = (kept, kept, block, block)
    if top > 2:
        bit = 2
        while bit < top:
            share = share + to_row(share, bit)
            bit *= 2
        own, *sent = call(give, gifts)(in_specs=[SMEM, VMEM, VMEM])(ids, solved, share)
    else:
        own, *sent = call(
            functools.partial(last_kernel, listed),
            gifts,
            [pltpu.VMEM(solved_shape.shape, f32), pltpu.VMEM(piece.shape, f32)],
            K["step"][S - 2],
        )(in_specs=[SMEM, SMEM] + [VMEM] * len(operands))(ids, lists[S - 2], *operands)
    near, far, both = [to_row(a, bit) for a, bit in zip(sent, (1, top, top + 1))]
    near, far, both = lax.optimization_barrier((near, far, both))
    quarters = [own, far, near, both]
    quarters += [to_core(a) for a in quarters]
    return call(
        functools.partial(place_kernel, quarter),
        shape((S, BS // 2, 4 * quarter), f32),
        [pltpu.VMEM((4 * quarter, BS), f32)],
    )(in_specs=[SMEM] + [VMEM] * 8)(ids, *quarters)


def solution(mesh):
    in_specs = (
        P("grp", ("row", "sub"), "rhs"),
        P("grp", ("row", "sub"), None),
        P("grp", ("row", "sub"), None),
        P("grp", "row", None),
    )
    out_specs = P("grp", ("row", "sub"), "rhs")
    step = functools.partial(body, mesh.shape["row"])
    return jax.shard_map(step, mesh=mesh, in_specs=in_specs, out_specs=out_specs, check_vma=False)
```

```python
import functools

import jax
import jax.numpy as jnp
from jax import lax
from jax.experimental import pallas as pl
from jax.experimental.pallas import tpu as pltpu
from jax.sharding import PartitionSpec as P

K = {'first': 0.3, 'prep': [2, 0, 0], 'step': [0, 0.1, 0], 'bulk': ['send', 'share0', 'share0'], 'swap': ['recv0', 'share1', 'share2'], 'rest': ['send', 'send', 'send'], 'groups': [[1], [2], [3]], 'meet': 1, 'early': 2, 'cut': [4, 4, 2]}
S = 4
BS = 128
LANES = 128
VMEM = pl.BlockSpec(memory_space=pltpu.VMEM)
SMEM = pl.BlockSpec(memory_space=pltpu.SMEM)


def split(a):
    high = a.astype(jnp.bfloat16)
    return high, (a - high.astype(jnp.float32)).astype(jnp.bfloat16)


def dot(a, b):
    return jnp.dot(a, b, preferred_element_type=jnp.float32)


def product(a, b_high, b_low):
    a_high, a_low = split(a)
    rows = a.shape[0]
    both = dot(jnp.concatenate([a_high, a_low], axis=0), b_high)
    return both[:rows] + both[rows:] + dot(a_high, b_low)


def call(kernel, outs, scratch=(), cost=0):
    return functools.partial(
        pl.pallas_call,
        kernel,
        out_shape=outs,
        scratch_shapes=list(scratch),
        compiler_params=pltpu.CompilerParams(vmem_limit_bytes=40 * 1024 * 1024),
        cost_estimate=pl.CostEstimate(flops=int(cost * 1e9), bytes_accessed=1000, transcendentals=0),
    )


def first_kernel(quarter, ids, lists, own, other, own_sides, other_sides, keep, send, turned, terms):
    blocks = own.shape[1] // BS
    turned[...] = jnp.concatenate([own_sides[0], other_sides[0]], axis=0).T
    sides = turned[pl.ds(pl.multiple_of(ids[0] * 2 * quarter, 2 * quarter), 2 * quarter), :]
    high, low = split(jnp.concatenate([own[...], other[...]], axis=0))
    share = product(sides, high, low)
    for i in range(blocks):
        terms[i] = share[:, i * BS : (i + 1) * BS]
    keep[...] = terms[:, pl.ds(pl.multiple_of(ids[1] * quarter, quarter), quarter), :]
    send[:blocks] = terms[:, pl.ds(pl.multiple_of((1 - ids[1]) * quarter, quarter), quarter), :]
    lane = lax.broadcasted_iota(jnp.int32, (quarter, BS), 1)
    told = jnp.zeros((quarter, BS), jnp.float32)
    for i in range(lists.shape[0]):
        for k in range(lists.shape[2]):
            told = jnp.where(lane == i * lists.shape[2] + k, lists[i, 0, k].astype(jnp.float32), told)
    send[blocks] = told


def prepare_kernel(quarter, place, ids, a0, a1, a2, *refs):
    a3 = jnp.concatenate([a[...] for a in refs[:-6]], axis=0)
    diag_high, diag_low, below_high, below_low, sides, turned = refs[-6:]
    width = diag_high.shape[1]
    depth = below_high.shape[1]
    first = pl.multiple_of(ids[0] * 2 * quarter + ids[1] * quarter, quarter)
    mine = slice(place * BS // 2, (place + 1) * BS // 2)
    for j, (one, two) in enumerate(((a0, a1), (a2, a3))):
        high, low = split(jnp.concatenate([one[mine, :width], two[mine, :width]], axis=0))
        diag_high[j * BS : (j + 1) * BS, :] = high
        diag_low[j * BS : (j + 1) * BS, :] = low
        below = jnp.concatenate([one[mine, width : width + depth], two[mine, width : width + depth]], axis=0)
        high, low = split(below.T)
        below_high[j] = high
        below_low[j] = low
        turned[...] = jnp.concatenate([one[mine, width + depth :], two[mine, width + depth :]], axis=0).T
        sides[j] = turned[pl.ds(first, quarter), :]


def advance(t, lists, told, stored, refs, solved):
    keep, recv, diag_high, diag_low, below_high, below_low, sides = refs
    before = solved.shape[0] - keep.shape[0]
    if before:
        solved[:before] = stored[0][...]
    solved[before:] = keep[...] + recv[...]
    listed = lists.shape[2]
    residuals = []
    for j in range(2):
        wanted = [told[t - 1, k] if j else lists[t - 1, 0, k] for k in range(listed)]
        picked = jnp.concatenate([solved[i] for i in wanted], axis=1)
        residuals.append(sides[j] - product(picked, below_high[j], below_low[j]))
    return product(jnp.concatenate(residuals, axis=1), diag_high[...], diag_low[...])


def step_kernel(t, lists, told, *refs):
    solved, share = refs[-2:]
    result = advance(t, lists, told, refs[:-9], refs[-9:-2], solved)
    for i in range(share.shape[0]):
        share[i] = result[:, i * BS : (i + 1) * BS]


def early_kernel(ids, solved, own, near):
    blocks = solved.shape[0] // own.shape[0]
    for t in range(own.shape[0]):
        own[t] = solved[t * blocks + ids[2]]
        near[t] = solved[t * blocks + ids[3]]


def give(first, ids, solved, share, own, near, far, both):
    blocks = share.shape[0]
    for t in range(first, S - 1):
        own[t - first] = solved[t * blocks + ids[2]]
        near[t - first] = solved[t * blocks + ids[3]]
    own[S - 1 - first] = share[ids[2]]
    near[S - 1 - first] = share[ids[3]]
    far[...] = share[ids[4]]
    both[...] = share[ids[5]]


def last_kernel(first, ids, lists, told, *refs):
    own, near, far, both, solved, share = refs[-6:]
    result = advance(S - 1, lists, told, refs[:-13], refs[-13:-6], solved)
    for i in range(share.shape[0]):
        share[i] = result[:, i * BS : (i + 1) * BS]
    give(first, ids, solved, share, own, near, far, both)


def place(quarter, ids, parts, whole):
    core, half = ids[0], ids[1]
    places = ((core, half), (core, 1 - half), (1 - core, half), (1 - core, 1 - half))
    for part, (c, h) in zip(parts, places):
        whole[pl.ds(pl.multiple_of((2 * c + h) * quarter, quarter), quarter), :] = part
    rows = whole.shape[1] // 2
    return jnp.where(core == 0, whole[:, :rows], whole[:, rows:]).T


def place_early_kernel(quarter, ids, a0, a1, a2, a3, out, whole):
    for t in range(out.shape[0]):
        out[t] = place(quarter, ids, (a0[t], a1[t], a2[t], a3[t]), whole)


def place_kernel(quarter, first, ids, *refs):
    quarters, out, whole = refs[:8], refs[-2], refs[-1]
    if first:
        out[:first] = refs[8][...]
    for t in range(first, S):
        parts = [quarters[2 * i][t - first] for i in range(4)]
        if t == S - 1:
            parts = [part + quarters[2 * i + 1][...] for i, part in enumerate(parts)]
        out[t] = place(quarter, ids, parts, whole)


def body(count, right_sides, diag_inverse, factor_below, block_lists):
    quarter = right_sides.shape[2] // 4
    blocks = diag_inverse.shape[2] // BS
    width = diag_inverse.shape[2]
    depth = factor_below.shape[2]
    listed = block_lists.shape[2]
    top = count // 2
    row, core = lax.axis_index("row"), lax.axis_index("sub")
    half = lax.rem(row, 2)
    team = row + 1 - 2 * half
    far = lax.rem(row + top, count)
    ids = jnp.stack([core, half, row, team, far, far + 1 - 2 * half]).astype(jnp.int32)

    def to_core(a):
        return lax.ppermute(a, "sub", [(0, 1), (1, 0)])

    def to_row(a, bit):
        return lax.ppermute(a, "row", [(i, i ^ bit) for i in range(count)])

    def after(a, *others):
        return lax.optimization_barrier((a, *others))[0]

    f32, bf16 = jnp.float32, jnp.bfloat16
    shape = jax.ShapeDtypeStruct
    piece = shape((blocks, quarter, BS), f32)

    def total(a):
        bit = 2
        while bit < top:
            a = a + to_row(a, bit)
            bit *= 2
        return a, to_row(a, top)

    def prepare(t, place, own, own_core, other, other_core):
        return call(
            functools.partial(prepare_kernel, quarter, place),
            (
                shape((2 * BS, width), bf16),
                shape((2 * BS, width), bf16),
                shape((2, depth, BS), bf16),
                shape((2, depth, BS), bf16),
                shape((2, quarter, BS), f32),
            ),
            [pltpu.VMEM((4 * quarter, BS), f32)],
            K["prep"][t - 1],
        )(in_specs=[SMEM] + [VMEM] * (3 + len(other_core)))(ids, own, own_core, other, *other_core)

    diag_first = diag_inverse[0]
    keep, send = call(
        functools.partial(first_kernel, quarter),
        (piece, shape((blocks + 1, quarter, BS), f32)),
        [pltpu.VMEM((4 * quarter, BS), f32), pltpu.VMEM((blocks, 2 * quarter, BS), f32)],
        K["first"],
    )(in_specs=[SMEM, SMEM, VMEM, VMEM, VMEM, VMEM])(
        ids, block_lists, diag_first, to_core(diag_first), right_sides, to_core(right_sides)
    )
    got = to_row(send, 1)

    groups = K["groups"]
    rest = []
    for g, group in enumerate(groups):
        diag, below, sides, _ = lax.optimization_barrier(
            (diag_inverse, factor_below, right_sides, {"first": diag_first, "send": send}[K["rest"][g]])
        )
        rows = [jnp.concatenate([diag[t], below[t - 1], sides[t]], axis=1) for t in group]
        rest.append(jnp.concatenate(rows, axis=0))
    rest_core = [to_core(a) for a in rest]

    share = keep + got[:blocks]
    told = got[blocks, 0, : (S - 1) * listed].reshape(S - 1, listed).astype(jnp.int32)

    gates = {"none": None, "send": send, "share0": share, "core1": rest_core[0]}
    stored, first = (), K["early"]
    others, other_cores = {}, {}

    def bulk():
        for u, name in enumerate(K["bulk"][: len(groups)]):
            if u not in others and name in gates:
                g = gates[name]
                others[u] = to_row(after(rest[u], g) if g is not None else rest[u], 1)

    for t in range(1, S):
        bulk()
        keep, recv = total(share)
        gates[f"recv{t - 1}"] = recv
        bulk()
        u = [t in group for group in groups].index(True)
        if u not in other_cores:
            g = K["swap"][u]
            gated = after(others[u], gates[g]) if g else others[u]
            rows = gated.shape[0] // K["cut"][u]
            other_cores[u] = [to_core(gated[i : i + rows]) for i in range(0, gated.shape[0], rows)]
        gates[f"other{t}"] = other_cores[u][-1]
        bulk()
        ready = prepare(t, groups[u].index(t), rest[u], rest_core[u], others[u], other_cores[u])
        operands = (*stored, keep, recv, *ready)
        gates[f"prep{t}"] = operands[-1]
        bulk()
        solved_shape = shape((t * blocks, quarter, BS), f32)
        if t < S - 1 or top > 2:
            solved, share = call(
                functools.partial(step_kernel, t), (solved_shape, piece), (), K["step"][t - 1]
            )(in_specs=[SMEM, SMEM] + [VMEM] * len(operands))(block_lists, told, *operands)
            stored = (solved,)
            gates[f"share{t}"] = share
            if t == S - 2 and first:
                early = shape((first, quarter, BS), f32)
                own, near = call(early_kernel, (early, early))(in_specs=[SMEM, VMEM])(ids, solved)
                near = to_row(near, 1)
                placed = call(
                    functools.partial(place_early_kernel, quarter),
                    shape((first, BS // 2, 4 * quarter), f32),
                    [pltpu.VMEM((4 * quarter, BS), f32)],
                )(in_specs=[SMEM] + [VMEM] * 4)(ids, own, near, to_core(own), to_core(near))

    block = shape((quarter, BS), f32)
    kept = shape((S - first, quarter, BS), f32)
    gifts = (kept, kept, block, block)
    if top > 2:
        bit = 2
        while bit < top:
            share = share + to_row(share, bit)
            bit *= 2
        own, *sent = call(functools.partial(give, first), gifts)(in_specs=[SMEM, VMEM, VMEM])(ids, solved, share)
    else:
        own, *sent = call(
            functools.partial(last_kernel, first),
            gifts,
            [pltpu.VMEM(solved_shape.shape, f32), pltpu.VMEM(piece.shape, f32)],
            K["step"][S - 2],
        )(in_specs=[SMEM] * 3 + [VMEM] * len(operands))(ids, block_lists, told, *operands)
    near, far, both = [to_row(a, bit) for a, bit in zip(sent, (1, top, top + 1))]
    if K["meet"]:
        near, far, both = lax.optimization_barrier((near, far, both))
    quarters = [own, far, near, both]
    quarters += [to_core(a) for a in quarters]
    if first:
        quarters.append(placed)
    return call(
        functools.partial(place_kernel, quarter, first),
        shape((S, BS // 2, 4 * quarter), f32),
        [pltpu.VMEM((4 * quarter, BS), f32)],
    )(in_specs=[SMEM] + [VMEM] * len(quarters))(ids, *quarters)


def solution(mesh):
    in_specs = (
        P("grp", ("row", "sub"), "rhs"),
        P("grp", ("row", "sub"), None),
        P("grp", ("row", "sub"), None),
        P("grp", "row", None),
    )
    out_specs = P("grp", ("row", "sub"), "rhs")
    step = functools.partial(body, mesh.shape["row"])
    return jax.shard_map(step, mesh=mesh, in_specs=in_specs, out_specs=out_specs, check_vma=False)
```

```python
import functools

import jax
import jax.numpy as jnp
from jax import lax
from jax.experimental import pallas as pl
from jax.experimental.pallas import tpu as pltpu
from jax.sharding import PartitionSpec as P

K = {'first': 0.3, 'prep': [2, 0, 0], 'step': [0, 0.1, 0], 'bulk': ['send', 'share0', 'share0'], 'swap': ['recv0', 'share1', 'share2'], 'rest': ['send', 'send', 'send'], 'groups': [[1], [2], [3]], 'meet': 1, 'early': 0, 'cut': [4, 4, 1]}
S = 4
BS = 128
LANES = 128
VMEM = pl.BlockSpec(memory_space=pltpu.VMEM)
SMEM = pl.BlockSpec(memory_space=pltpu.SMEM)


def split(a):
    high = a.astype(jnp.bfloat16)
    return high, (a - high.astype(jnp.float32)).astype(jnp.bfloat16)


def dot(a, b):
    return jnp.dot(a, b, preferred_element_type=jnp.float32)


def product(a, b_high, b_low):
    a_high, a_low = split(a)
    rows = a.shape[0]
    both = dot(jnp.concatenate([a_high, a_low], axis=0), b_high)
    return both[:rows] + both[rows:] + dot(a_high, b_low)


def call(kernel, outs, scratch=(), cost=0):
    return functools.partial(
        pl.pallas_call,
        kernel,
        out_shape=outs,
        scratch_shapes=list(scratch),
        compiler_params=pltpu.CompilerParams(vmem_limit_bytes=40 * 1024 * 1024),
        cost_estimate=pl.CostEstimate(flops=int(cost * 1e9), bytes_accessed=1000, transcendentals=0),
    )


def first_kernel(quarter, ids, lists, own, other, own_sides, other_sides, keep, send, turned, terms):
    blocks = own.shape[1] // BS
    turned[...] = jnp.concatenate([own_sides[0], other_sides[0]], axis=0).T
    sides = turned[pl.ds(pl.multiple_of(ids[0] * 2 * quarter, 2 * quarter), 2 * quarter), :]
    high, low = split(jnp.concatenate([own[...], other[...]], axis=0))
    share = product(sides, high, low)
    for i in range(blocks):
        terms[i] = share[:, i * BS : (i + 1) * BS]
    keep[...] = terms[:, pl.ds(pl.multiple_of(ids[1] * quarter, quarter), quarter), :]
    away = pl.ds(pl.multiple_of((1 - ids[1]) * quarter, quarter), quarter)
    for i in range(blocks):
        send[i * quarter : (i + 1) * quarter] = terms[i, away, :]
    lane = lax.broadcasted_iota(jnp.int32, (8, BS), 1)
    told = jnp.zeros((8, BS), jnp.float32)
    for i in range(lists.shape[0]):
        for k in range(lists.shape[2]):
            told = jnp.where(lane == i * lists.shape[2] + k, lists[i, 0, k].astype(jnp.float32), told)
    send[blocks * quarter :] = told


def prepare_kernel(quarter, place, ids, a0, a1, a2, *refs):
    a3 = jnp.concatenate([a[...] for a in refs[:-6]], axis=0)
    diag_high, diag_low, below_high, below_low, sides, turned = refs[-6:]
    width = diag_high.shape[1]
    depth = below_high.shape[1]
    first = pl.multiple_of(ids[0] * 2 * quarter + ids[1] * quarter, quarter)
    mine = slice(place * BS // 2, (place + 1) * BS // 2)
    for j, (one, two) in enumerate(((a0, a1), (a2, a3))):
        high, low = split(jnp.concatenate([one[mine, :width], two[mine, :width]], axis=0))
        diag_high[j * BS : (j + 1) * BS, :] = high
        diag_low[j * BS : (j + 1) * BS, :] = low
        below = jnp.concatenate([one[mine, width : width + depth], two[mine, width : width + depth]], axis=0)
        high, low = split(below.T)
        below_high[j] = high
        below_low[j] = low
        turned[...] = jnp.concatenate([one[mine, width + depth :], two[mine, width + depth :]], axis=0).T
        sides[j] = turned[pl.ds(first, quarter), :]


def advance(t, lists, told, stored, refs, solved):
    keep, recv, diag_high, diag_low, below_high, below_low, sides = refs
    before = solved.shape[0] - keep.shape[0]
    if before:
        solved[:before] = stored[0][...]
    solved[before:] = keep[...] + recv[...]
    listed = lists.shape[2]
    residuals = []
    for j in range(2):
        wanted = [told[t - 1, k] if j else lists[t - 1, 0, k] for k in range(listed)]
        picked = jnp.concatenate([solved[i] for i in wanted], axis=1)
        residuals.append(sides[j] - product(picked, below_high[j], below_low[j]))
    return product(jnp.concatenate(residuals, axis=1), diag_high[...], diag_low[...])


def step_kernel(t, lists, told, *refs):
    solved, share = refs[-2:]
    result = advance(t, lists, told, refs[:-9], refs[-9:-2], solved)
    for i in range(share.shape[0]):
        share[i] = result[:, i * BS : (i + 1) * BS]


def early_kernel(ids, solved, own, near):
    blocks = solved.shape[0] // own.shape[0]
    for t in range(own.shape[0]):
        own[t] = solved[t * blocks + ids[2]]
        near[t] = solved[t * blocks + ids[3]]


def give(first, ids, solved, share, own, near, far, both):
    blocks = share.shape[0]
    for t in range(first, S - 1):
        own[t - first] = solved[t * blocks + ids[2]]
        near[t - first] = solved[t * blocks + ids[3]]
    own[S - 1 - first] = share[ids[2]]
    near[S - 1 - first] = share[ids[3]]
    far[...] = share[ids[4]]
    both[...] = share[ids[5]]


def last_kernel(first, ids, lists, told, *refs):
    own, near, far, both, solved, share = refs[-6:]
    result = advance(S - 1, lists, told, refs[:-13], refs[-13:-6], solved)
    for i in range(share.shape[0]):
        share[i] = result[:, i * BS : (i + 1) * BS]
    give(first, ids, solved, share, own, near, far, both)


def place(quarter, ids, parts, whole):
    core, half = ids[0], ids[1]
    places = ((core, half), (core, 1 - half), (1 - core, half), (1 - core, 1 - half))
    for part, (c, h) in zip(parts, places):
        whole[pl.ds(pl.multiple_of((2 * c + h) * quarter, quarter), quarter), :] = part
    rows = whole.shape[1] // 2
    return jnp.where(core == 0, whole[:, :rows], whole[:, rows:]).T


def place_kernel(quarter, first, ids, *refs):
    quarters, early, out, whole = refs[:8], refs[8:-2], refs[-2], refs[-1]
    for t in range(S):
        if t < first:
            parts = [a[t] for a in early]
        else:
            parts = [quarters[2 * i][t - first] for i in range(4)]
        if t == S - 1:
            parts = [part + quarters[2 * i + 1][...] for i, part in enumerate(parts)]
        out[t] = place(quarter, ids, parts, whole)


def body(count, right_sides, diag_inverse, factor_below, block_lists):
    quarter = right_sides.shape[2] // 4
    blocks = diag_inverse.shape[2] // BS
    width = diag_inverse.shape[2]
    depth = factor_below.shape[2]
    listed = block_lists.shape[2]
    top = count // 2
    row, core = lax.axis_index("row"), lax.axis_index("sub")
    half = lax.rem(row, 2)
    team = row + 1 - 2 * half
    far = lax.rem(row + top, count)
    ids = jnp.stack([core, half, row, team, far, far + 1 - 2 * half]).astype(jnp.int32)

    def to_core(a):
        return lax.ppermute(a, "sub", [(0, 1), (1, 0)])

    def to_row(a, bit):
        return lax.ppermute(a, "row", [(i, i ^ bit) for i in range(count)])

    def after(a, *others):
        return lax.optimization_barrier((a, *others))[0]

    f32, bf16 = jnp.float32, jnp.bfloat16
    shape = jax.ShapeDtypeStruct
    piece = shape((blocks, quarter, BS), f32)

    def total(a):
        bit = 2
        while bit < top:
            a = a + to_row(a, bit)
            bit *= 2
        return a, to_row(a, top)

    def prepare(t, place, own, own_core, other, other_core):
        return call(
            functools.partial(prepare_kernel, quarter, place),
            (
                shape((2 * BS, width), bf16),
                shape((2 * BS, width), bf16),
                shape((2, depth, BS), bf16),
                shape((2, depth, BS), bf16),
                shape((2, quarter, BS), f32),
            ),
            [pltpu.VMEM((4 * quarter, BS), f32)],
            K["prep"][t - 1],
        )(in_specs=[SMEM] + [VMEM] * (3 + len(other_core)))(ids, own, own_core, other, *other_core)

    diag_first = diag_inverse[0]
    keep, send = call(
        functools.partial(first_kernel, quarter),
        (piece, shape((blocks * quarter + 8, BS), f32)),
        [pltpu.VMEM((4 * quarter, BS), f32), pltpu.VMEM((blocks, 2 * quarter, BS), f32)],
        K["first"],
    )(in_specs=[SMEM, SMEM, VMEM, VMEM, VMEM, VMEM])(
        ids, block_lists, diag_first, to_core(diag_first), right_sides, to_core(right_sides)
    )
    got = to_row(send, 1)

    groups = K["groups"]
    rest = []
    for g, group in enumerate(groups):
        diag, below, sides, _ = lax.optimization_barrier(
            (diag_inverse, factor_below, right_sides, {"first": diag_first, "send": send}[K["rest"][g]])
        )
        rows = [jnp.concatenate([diag[t], below[t - 1], sides[t]], axis=1) for t in group]
        rest.append(jnp.concatenate(rows, axis=0))
    rest_core = [to_core(a) for a in rest]

    share = keep + got[: blocks * quarter].reshape(blocks, quarter, BS)
    told = got[blocks * quarter, : (S - 1) * listed].reshape(S - 1, listed).astype(jnp.int32)

    gates = {"none": None, "send": send, "share0": share, "core1": rest_core[0]}
    stored, first = (), K["early"]
    others, other_cores = {}, {}

    def bulk():
        for u, name in enumerate(K["bulk"][: len(groups)]):
            if u not in others and name in gates:
                g = gates[name]
                others[u] = to_row(after(rest[u], g) if g is not None else rest[u], 1)

    for t in range(1, S):
        bulk()
        keep, recv = total(share)
        gates[f"recv{t - 1}"] = recv
        bulk()
        u = [t in group for group in groups].index(True)
        if u not in other_cores:
            g = K["swap"][u]
            gated = after(others[u], gates[g]) if g else others[u]
            rows = gated.shape[0] // K["cut"][u]
            other_cores[u] = [to_core(gated[i : i + rows]) for i in range(0, gated.shape[0], rows)]
        gates[f"other{t}"] = other_cores[u][-1]
        bulk()
        ready = prepare(t, groups[u].index(t), rest[u], rest_core[u], others[u], other_cores[u])
        operands = (*stored, keep, recv, *ready)
        gates[f"prep{t}"] = operands[-1]
        bulk()
        solved_shape = shape((t * blocks, quarter, BS), f32)
        if t < S - 1 or top > 2:
            solved, share = call(
                functools.partial(step_kernel, t), (solved_shape, piece), (), K["step"][t - 1]
            )(in_specs=[SMEM, SMEM] + [VMEM] * len(operands))(block_lists, told, *operands)
            stored = (solved,)
            gates[f"share{t}"] = share
            if t == S - 2 and first:
                early = shape((first, quarter, BS), f32)
                early_kept, near = call(early_kernel, (early, early))(in_specs=[SMEM, VMEM])(ids, solved)
                near = to_row(near, 1)
                placed = [early_kept, near, to_core(early_kept), to_core(near)]

    block = shape((quarter, BS), f32)
    kept = shape((S - first, quarter, BS), f32)
    gifts = (kept, kept, block, block)
    if top > 2:
        bit = 2
        while bit < top:
            share = share + to_row(share, bit)
            bit *= 2
        own, *sent = call(functools.partial(give, first), gifts)(in_specs=[SMEM, VMEM, VMEM])(ids, solved, share)
    else:
        own, *sent = call(
            functools.partial(last_kernel, first),
            gifts,
            [pltpu.VMEM(solved_shape.shape, f32), pltpu.VMEM(piece.shape, f32)],
            K["step"][S - 2],
        )(in_specs=[SMEM] * 3 + [VMEM] * len(operands))(ids, block_lists, told, *operands)
    near, far, both = [to_row(a, bit) for a, bit in zip(sent, (1, top, top + 1))]
    if K["meet"]:
        near, far, both = lax.optimization_barrier((near, far, both))
    quarters = [own, far, near, both]
    quarters += [to_core(a) for a in quarters]
    if first:
        quarters += placed
    return call(
        functools.partial(place_kernel, quarter, first),
        shape((S, BS // 2, 4 * quarter), f32),
        [pltpu.VMEM((4 * quarter, BS), f32)],
    )(in_specs=[SMEM] + [VMEM] * len(quarters))(ids, *quarters)


def solution(mesh):
    in_specs = (
        P("grp", ("row", "sub"), "rhs"),
        P("grp", ("row", "sub"), None),
        P("grp", ("row", "sub"), None),
        P("grp", "row", None),
    )
    out_specs = P("grp", ("row", "sub"), "rhs")
    step = functools.partial(body, mesh.shape["row"])
    return jax.shard_map(step, mesh=mesh, in_specs=in_specs, out_specs=out_specs, check_vma=False)
```

```python
import functools

import jax
import jax.numpy as jnp
from jax import lax
from jax.experimental import pallas as pl
from jax.experimental.pallas import tpu as pltpu
from jax.sharding import PartitionSpec as P

K = {'first': 0.3, 'prep': [2, 0, 0], 'step': [0, 0.1, 0], 'bulk': ['send', 'share0', 'share0'], 'swap': ['recv0', 'share1', 'share2'], 'rest': ['send', 'send', 'send'], 'groups': [[1], [2], [3]], 'meet': 0, 'early': 2, 'cut': [4, 4, 1]}
S = 4
BS = 128
LANES = 128
VMEM = pl.BlockSpec(memory_space=pltpu.VMEM)
SMEM = pl.BlockSpec(memory_space=pltpu.SMEM)


def split(a):
    high = a.astype(jnp.bfloat16)
    return high, (a - high.astype(jnp.float32)).astype(jnp.bfloat16)


def dot(a, b):
    return jnp.dot(a, b, preferred_element_type=jnp.float32)


def product(a, b_high, b_low):
    a_high, a_low = split(a)
    rows = a.shape[0]
    both = dot(jnp.concatenate([a_high, a_low], axis=0), b_high)
    return both[:rows] + both[rows:] + dot(a_high, b_low)


def call(kernel, outs, scratch=(), cost=0):
    return functools.partial(
        pl.pallas_call,
        kernel,
        out_shape=outs,
        scratch_shapes=list(scratch),
        compiler_params=pltpu.CompilerParams(vmem_limit_bytes=40 * 1024 * 1024),
        cost_estimate=pl.CostEstimate(flops=int(cost * 1e9), bytes_accessed=1000, transcendentals=0),
    )


def first_kernel(quarter, ids, lists, own, other, own_sides, other_sides, keep, send, turned, terms):
    blocks = own.shape[1] // BS
    turned[...] = jnp.concatenate([own_sides[0], other_sides[0]], axis=0).T
    sides = turned[pl.ds(pl.multiple_of(ids[0] * 2 * quarter, 2 * quarter), 2 * quarter), :]
    high, low = split(jnp.concatenate([own[...], other[0]], axis=0))
    share = product(sides, high, low)
    for i in range(blocks):
        terms[i] = share[:, i * BS : (i + 1) * BS]
    keep[...] = terms[:, pl.ds(pl.multiple_of(ids[1] * quarter, quarter), quarter), :]
    away = pl.ds(pl.multiple_of((1 - ids[1]) * quarter, quarter), quarter)
    for i in range(blocks):
        send[i * quarter : (i + 1) * quarter] = terms[i, away, :]
    lane = lax.broadcasted_iota(jnp.int32, (8, BS), 1)
    told = jnp.zeros((8, BS), jnp.float32)
    for i in range(lists.shape[0]):
        for k in range(lists.shape[2]):
            told = jnp.where(lane == i * lists.shape[2] + k, lists[i, 0, k].astype(jnp.float32), told)
    send[blocks * quarter :] = told


def prepare_kernel(quarter, place, ids, a0, a1, a2, *refs):
    a3 = jnp.concatenate([a[...] for a in refs[:-6]], axis=0)
    diag_high, diag_low, below_high, below_low, sides, turned = refs[-6:]
    width = diag_high.shape[1]
    depth = below_high.shape[1]
    first = pl.multiple_of(ids[0] * 2 * quarter + ids[1] * quarter, quarter)
    mine = slice(place * BS // 2, (place + 1) * BS // 2)
    for j, (one, two) in enumerate(((a0, a1), (a2, a3))):
        high, low = split(jnp.concatenate([one[mine, :width], two[mine, :width]], axis=0))
        diag_high[j * BS : (j + 1) * BS, :] = high
        diag_low[j * BS : (j + 1) * BS, :] = low
        below = jnp.concatenate([one[mine, width : width + depth], two[mine, width : width + depth]], axis=0)
        high, low = split(below.T)
        below_high[j] = high
        below_low[j] = low
        turned[...] = jnp.concatenate([one[mine, width + depth :], two[mine, width + depth :]], axis=0).T
        sides[j] = turned[pl.ds(first, quarter), :]


def advance(t, lists, told, stored, refs, solved):
    keep, recv, diag_high, diag_low, below_high, below_low, sides = refs
    before = solved.shape[0] - keep.shape[0]
    if before:
        solved[:before] = stored[0][...]
    solved[before:] = keep[...] + recv[...]
    listed = lists.shape[2]
    residuals = []
    for j in range(2):
        wanted = [told[t - 1, k] if j else lists[t - 1, 0, k] for k in range(listed)]
        picked = jnp.concatenate([solved[i] for i in wanted], axis=1)
        residuals.append(sides[j] - product(picked, below_high[j], below_low[j]))
    return product(jnp.concatenate(residuals, axis=1), diag_high[...], diag_low[...])


def step_kernel(t, lists, told, *refs):
    solved, share = refs[-2:]
    result = advance(t, lists, told, refs[:-9], refs[-9:-2], solved)
    for i in range(share.shape[0]):
        share[i] = result[:, i * BS : (i + 1) * BS]


def whole_step_kernel(quarter, place, t, pieces, ids, lists, told, *refs):
    taken, rest, between = refs[: 3 + pieces], refs[3 + pieces : -6], refs[-6:]
    prepare_kernel(quarter, place, ids, *taken, *between)
    step_kernel(t, lists, told, *rest[:-2], *between[:-1], *rest[-2:])


def early_kernel(ids, solved, own, near):
    blocks = solved.shape[0] // own.shape[0]
    for t in range(own.shape[0]):
        own[t] = solved[t * blocks + ids[2]]
        near[t] = solved[t * blocks + ids[3]]


def give(first, ids, solved, share, own, near, far, both):
    blocks = share.shape[0]
    for t in range(first, S - 1):
        own[t - first] = solved[t * blocks + ids[2]]
        near[t - first] = solved[t * blocks + ids[3]]
    own[S - 1 - first] = share[ids[2]]
    near[S - 1 - first] = share[ids[3]]
    far[...] = share[ids[4]]
    both[...] = share[ids[5]]


def last_kernel(first, ids, lists, told, *refs):
    own, near, far, both, solved, share = refs[-6:]
    result = advance(S - 1, lists, told, refs[:-13], refs[-13:-6], solved)
    for i in range(share.shape[0]):
        share[i] = result[:, i * BS : (i + 1) * BS]
    give(first, ids, solved, share, own, near, far, both)


def place(quarter, ids, parts, whole):
    core, half = ids[0], ids[1]
    places = ((core, half), (core, 1 - half), (1 - core, half), (1 - core, 1 - half))
    for part, (c, h) in zip(parts, places):
        whole[pl.ds(pl.multiple_of((2 * c + h) * quarter, quarter), quarter), :] = part
    rows = whole.shape[1] // 2
    return jnp.where(core == 0, whole[:, :rows], whole[:, rows:]).T


def place_kernel(quarter, first, ids, *refs):
    quarters, early, out, whole = refs[:8], refs[8:-2], refs[-2], refs[-1]
    for t in range(S):
        if t < first:
            parts = [a[t] for a in early]
        else:
            parts = [quarters[2 * i][t - first] for i in range(4)]
        if t == S - 1:
            parts = [part + quarters[2 * i + 1][...] for i, part in enumerate(parts)]
        out[t] = place(quarter, ids, parts, whole.at[t])


def body(count, right_sides, diag_inverse, factor_below, block_lists):
    quarter = right_sides.shape[2] // 4
    blocks = diag_inverse.shape[2] // BS
    width = diag_inverse.shape[2]
    depth = factor_below.shape[2]
    listed = block_lists.shape[2]
    top = count // 2
    row, core = lax.axis_index("row"), lax.axis_index("sub")
    half = lax.rem(row, 2)
    team = row + 1 - 2 * half
    far = lax.rem(row + top, count)
    ids = jnp.stack([core, half, row, team, far, far + 1 - 2 * half]).astype(jnp.int32)

    def to_core(a):
        return lax.ppermute(a, "sub", [(0, 1), (1, 0)])

    def to_row(a, bit):
        return lax.ppermute(a, "row", [(i, i ^ bit) for i in range(count)])

    def after(a, *others):
        return lax.optimization_barrier((a, *others))[0]

    f32, bf16 = jnp.float32, jnp.bfloat16
    shape = jax.ShapeDtypeStruct
    piece = shape((blocks, quarter, BS), f32)

    def total(a):
        bit = 2
        while bit < top:
            a = a + to_row(a, bit)
            bit *= 2
        return a, to_row(a, top)

    ready_shapes = (
        shape((2 * BS, width), bf16),
        shape((2 * BS, width), bf16),
        shape((2, depth, BS), bf16),
        shape((2, depth, BS), bf16),
        shape((2, quarter, BS), f32),
    )

    def prepare(t, place, own, own_core, other, other_core):
        return call(
            functools.partial(prepare_kernel, quarter, place),
            ready_shapes,
            [pltpu.VMEM((4 * quarter, BS), f32)],
            K["prep"][t - 1],
        )(in_specs=[SMEM] + [VMEM] * (3 + len(other_core)))(ids, own, own_core, other, *other_core)

    diag_first = diag_inverse[0]
    keep, send = call(
        functools.partial(first_kernel, quarter),
        (piece, shape((blocks * quarter + 8, BS), f32)),
        [pltpu.VMEM((4 * quarter, BS), f32), pltpu.VMEM((blocks, 2 * quarter, BS), f32)],
        K["first"],
    )(in_specs=[SMEM, SMEM, VMEM, VMEM, VMEM, VMEM])(
        ids, block_lists, diag_first, to_core(diag_inverse), right_sides, to_core(right_sides)
    )
    got = to_row(send, 1)

    groups = K["groups"]
    rest = []
    for g, group in enumerate(groups):
        diag, below, sides, _ = lax.optimization_barrier(
            (diag_inverse, factor_below, right_sides, {"first": diag_first, "send": send}[K["rest"][g]])
        )
        rows = [jnp.concatenate([diag[t], below[t - 1], sides[t]], axis=1) for t in group]
        rest.append(jnp.concatenate(rows, axis=0))
    rest_core = [to_core(a) for a in rest]

    share = keep + got[: blocks * quarter].reshape(blocks, quarter, BS)
    told = got[blocks * quarter, : (S - 1) * listed].reshape(S - 1, listed).astype(jnp.int32)

    gates = {"none": None, "send": send, "share0": share, "core1": rest_core[0]}
    stored, first = (), K["early"]
    others, other_cores = {}, {}

    def bulk():
        for u, name in enumerate(K["bulk"][: len(groups)]):
            if u not in others and name in gates:
                g = gates[name]
                others[u] = to_row(after(rest[u], g) if g is not None else rest[u], 1)

    for t in range(1, S):
        bulk()
        keep, recv = total(share)
        gates[f"recv{t - 1}"] = recv
        bulk()
        u = [t in group for group in groups].index(True)
        if u not in other_cores:
            g = K["swap"][u]
            gated = after(others[u], gates[g]) if g else others[u]
            rows = gated.shape[0] // K["cut"][u]
            other_cores[u] = [to_core(gated[i : i + rows]) for i in range(0, gated.shape[0], rows)]
        gates[f"other{t}"] = other_cores[u][-1]
        bulk()
        if t == 1 and top == 2:
            pieces = other_cores[u]
            operands = (rest[u], rest_core[u], others[u], *pieces, keep, recv)
            kernel = functools.partial(whole_step_kernel, quarter, groups[u].index(t), t, len(pieces))
            solved, share = call(
                kernel,
                (shape((blocks, quarter, BS), f32), piece),
                [pltpu.VMEM(a.shape, a.dtype) for a in ready_shapes] + [pltpu.VMEM((4 * quarter, BS), f32)],
                K["step"][0],
            )(in_specs=[SMEM] * 3 + [VMEM] * len(operands))(ids, block_lists, told, *operands)
            stored = (solved,)
            gates["share1"] = share
            continue
        ready = prepare(t, groups[u].index(t), rest[u], rest_core[u], others[u], other_cores[u])
        operands = (*stored, keep, recv, *ready)
        gates[f"prep{t}"] = operands[-1]
        bulk()
        solved_shape = shape((t * blocks, quarter, BS), f32)
        if t < S - 1 or top > 2:
            solved, share = call(
                functools.partial(step_kernel, t), (solved_shape, piece), (), K["step"][t - 1]
            )(in_specs=[SMEM, SMEM] + [VMEM] * len(operands))(block_lists, told, *operands)
            stored = (solved,)
            gates[f"share{t}"] = share
            if t == S - 2 and first:
                early = shape((first, quarter, BS), f32)
                early_kept, near = call(early_kernel, (early, early))(in_specs=[SMEM, VMEM])(ids, solved)
                near = to_row(near, 1)
                placed = [early_kept, near, to_core(early_kept), to_core(near)]

    block = shape((quarter, BS), f32)
    kept = shape((S - first, quarter, BS), f32)
    gifts = (kept, kept, block, block)
    if top > 2:
        bit = 2
        while bit < top:
            share = share + to_row(share, bit)
            bit *= 2
        own, *sent = call(functools.partial(give, first), gifts)(in_specs=[SMEM, VMEM, VMEM])(ids, solved, share)
    else:
        own, *sent = call(
            functools.partial(last_kernel, first),
            gifts,
            [pltpu.VMEM(solved_shape.shape, f32), pltpu.VMEM(piece.shape, f32)],
            K["step"][S - 2],
        )(in_specs=[SMEM] * 3 + [VMEM] * len(operands))(ids, block_lists, told, *operands)
    near, far, both = [to_row(a, bit) for a, bit in zip(sent, (1, top, top + 1))]
    if K["meet"]:
        near, far, both = lax.optimization_barrier((near, far, both))
    quarters = [own, far, near, both]
    quarters += [to_core(a) for a in quarters]
    if first:
        quarters += placed
    return call(
        functools.partial(place_kernel, quarter, first),
        shape((S, BS // 2, 4 * quarter), f32),
        [pltpu.VMEM((S, 4 * quarter, BS), f32)],
    )(in_specs=[SMEM] + [VMEM] * len(quarters))(ids, *quarters)


def solution(mesh):
    in_specs = (
        P("grp", ("row", "sub"), "rhs"),
        P("grp", ("row", "sub"), None),
        P("grp", ("row", "sub"), None),
        P("grp", "row", None),
    )
    out_specs = P("grp", ("row", "sub"), "rhs")
    step = functools.partial(body, mesh.shape["row"])
    return jax.shard_map(step, mesh=mesh, in_specs=in_specs, out_specs=out_specs, check_vma=False)
```

```python
import functools

import jax
import jax.numpy as jnp
from jax import lax
from jax.experimental import pallas as pl
from jax.experimental.pallas import tpu as pltpu
from jax.sharding import PartitionSpec as P

K = {'first': 0.3, 'prep': [2, 0, 0], 'step': [0, 0.1, 0], 'bulk': ['none', 'share0', 'share0'], 'swap': ['recv0', 'share1', 'share2'], 'rest': ['send', 'send', 'send'], 'groups': [[1], [2], [3]], 'meet': 0, 'early': 2, 'cut': [4, 2, 4]}
S = 4
BS = 128
LANES = 128
VMEM = pl.BlockSpec(memory_space=pltpu.VMEM)
SMEM = pl.BlockSpec(memory_space=pltpu.SMEM)


def split(a):
    high = a.astype(jnp.bfloat16)
    return high, (a - high.astype(jnp.float32)).astype(jnp.bfloat16)


def dot(a, b):
    return jnp.dot(a, b, preferred_element_type=jnp.float32)


def product(a, b_high, b_low):
    a_high, a_low = split(a)
    rows = a.shape[0]
    both = dot(jnp.concatenate([a_high, a_low], axis=0), b_high)
    return both[:rows] + both[rows:] + dot(a_high, b_low)


def call(kernel, outs, scratch=(), cost=0):
    return functools.partial(
        pl.pallas_call,
        kernel,
        out_shape=outs,
        scratch_shapes=list(scratch),
        compiler_params=pltpu.CompilerParams(vmem_limit_bytes=40 * 1024 * 1024),
        cost_estimate=pl.CostEstimate(flops=int(cost * 1e9), bytes_accessed=1000, transcendentals=0),
    )


def first_kernel(quarter, ids, lists, own, other, own_sides, other_sides, keep, send, turned, terms):
    blocks = own.shape[1] // BS
    turned[...] = jnp.concatenate([own_sides[0], other_sides[0]], axis=0).T
    sides = turned[pl.ds(pl.multiple_of(ids[0] * 2 * quarter, 2 * quarter), 2 * quarter), :]
    high, low = split(jnp.concatenate([own[...], other[0]], axis=0))
    share = product(sides, high, low)
    for i in range(blocks):
        terms[i] = share[:, i * BS : (i + 1) * BS]
    keep[...] = terms[:, pl.ds(pl.multiple_of(ids[1] * quarter, quarter), quarter), :]
    away = pl.ds(pl.multiple_of((1 - ids[1]) * quarter, quarter), quarter)
    for i in range(blocks):
        send[i * quarter : (i + 1) * quarter] = terms[i, away, :]
    lane = lax.broadcasted_iota(jnp.int32, (8, BS), 1)
    told = jnp.zeros((8, BS), jnp.float32)
    for i in range(lists.shape[0]):
        for k in range(lists.shape[2]):
            told = jnp.where(lane == i * lists.shape[2] + k, lists[i, 0, k].astype(jnp.float32), told)
    send[blocks * quarter :] = told


def prepare_kernel(quarter, place, ids, a0, a1, a2, *refs):
    a3 = jnp.concatenate([a[...] for a in refs[:-6]], axis=0)
    diag_high, diag_low, below_high, below_low, sides, turned = refs[-6:]
    width = diag_high.shape[1]
    depth = below_high.shape[1]
    first = pl.multiple_of(ids[0] * 2 * quarter + ids[1] * quarter, quarter)
    mine = slice(place * BS // 2, (place + 1) * BS // 2)
    for j, (one, two) in enumerate(((a0, a1), (a2, a3))):
        high, low = split(jnp.concatenate([one[mine, :width], two[mine, :width]], axis=0))
        diag_high[j * BS : (j + 1) * BS, :] = high
        diag_low[j * BS : (j + 1) * BS, :] = low
        below = jnp.concatenate([one[mine, width : width + depth], two[mine, width : width + depth]], axis=0)
        high, low = split(below.T)
        below_high[j] = high
        below_low[j] = low
        turned[...] = jnp.concatenate([one[mine, width + depth :], two[mine, width + depth :]], axis=0).T
        sides[j] = turned[pl.ds(first, quarter), :]


def advance(t, lists, told, stored, refs, solved):
    keep, recv, diag_high, diag_low, below_high, below_low, sides = refs
    before = solved.shape[0] - keep.shape[0]
    if before:
        solved[:before] = stored[0][...]
    solved[before:] = keep[...] + recv[...]
    listed = lists.shape[2]
    residuals = []
    for j in range(2):
        wanted = [told[t - 1, k] if j else lists[t - 1, 0, k] for k in range(listed)]
        picked = jnp.concatenate([solved[i] for i in wanted], axis=1)
        residuals.append(sides[j] - product(picked, below_high[j], below_low[j]))
    return product(jnp.concatenate(residuals, axis=1), diag_high[...], diag_low[...])


def step_kernel(t, lists, told, *refs):
    solved, share = refs[-2:]
    result = advance(t, lists, told, refs[:-9], refs[-9:-2], solved)
    for i in range(share.shape[0]):
        share[i] = result[:, i * BS : (i + 1) * BS]


def whole_step_kernel(quarter, place, t, pieces, ids, lists, told, *refs):
    taken, rest, between = refs[: 3 + pieces], refs[3 + pieces : -6], refs[-6:]
    prepare_kernel(quarter, place, ids, *taken, *between)
    step_kernel(t, lists, told, *rest[:-2], *between[:-1], *rest[-2:])


def early_kernel(ids, solved, own, near):
    blocks = solved.shape[0] // own.shape[0]
    for t in range(own.shape[0]):
        own[t] = solved[t * blocks + ids[2]]
        near[t] = solved[t * blocks + ids[3]]


def give(first, ids, solved, share, own, near, far, both):
    blocks = share.shape[0]
    for t in range(first, S - 1):
        own[t - first] = solved[t * blocks + ids[2]]
        near[t - first] = solved[t * blocks + ids[3]]
    own[S - 1 - first] = share[ids[2]]
    near[S - 1 - first] = share[ids[3]]
    far[...] = share[ids[4]]
    both[...] = share[ids[5]]


def last_kernel(first, ids, lists, told, *refs):
    own, near, far, both, solved, share = refs[-6:]
    result = advance(S - 1, lists, told, refs[:-13], refs[-13:-6], solved)
    for i in range(share.shape[0]):
        share[i] = result[:, i * BS : (i + 1) * BS]
    give(first, ids, solved, share, own, near, far, both)


def place(quarter, ids, parts, whole):
    core, half = ids[0], ids[1]
    places = ((core, half), (core, 1 - half), (1 - core, half), (1 - core, 1 - half))
    for part, (c, h) in zip(parts, places):
        whole[pl.ds(pl.multiple_of((2 * c + h) * quarter, quarter), quarter), :] = part
    rows = whole.shape[1] // 2
    return jnp.where(core == 0, whole[:, :rows], whole[:, rows:]).T


def place_kernel(quarter, first, ids, *refs):
    quarters, early, out, whole = refs[:8], refs[8:-2], refs[-2], refs[-1]
    for t in range(S):
        if t < first:
            parts = [a[t] for a in early]
        else:
            parts = [quarters[2 * i][t - first] for i in range(4)]
        if t == S - 1:
            parts = [part + quarters[2 * i + 1][...] for i, part in enumerate(parts)]
        out[t] = place(quarter, ids, parts, whole.at[t])


def body(count, right_sides, diag_inverse, factor_below, block_lists):
    quarter = right_sides.shape[2] // 4
    blocks = diag_inverse.shape[2] // BS
    width = diag_inverse.shape[2]
    depth = factor_below.shape[2]
    listed = block_lists.shape[2]
    top = count // 2
    row, core = lax.axis_index("row"), lax.axis_index("sub")
    half = lax.rem(row, 2)
    team = row + 1 - 2 * half
    far = lax.rem(row + top, count)
    ids = jnp.stack([core, half, row, team, far, far + 1 - 2 * half]).astype(jnp.int32)

    def to_core(a):
        return lax.ppermute(a, "sub", [(0, 1), (1, 0)])

    def to_row(a, bit):
        return lax.ppermute(a, "row", [(i, i ^ bit) for i in range(count)])

    def after(a, *others):
        return lax.optimization_barrier((a, *others))[0]

    f32, bf16 = jnp.float32, jnp.bfloat16
    shape = jax.ShapeDtypeStruct
    piece = shape((blocks, quarter, BS), f32)

    def total(a):
        bit = 2
        while bit < top:
            a = a + to_row(a, bit)
            bit *= 2
        return a, to_row(a, top)

    ready_shapes = (
        shape((2 * BS, width), bf16),
        shape((2 * BS, width), bf16),
        shape((2, depth, BS), bf16),
        shape((2, depth, BS), bf16),
        shape((2, quarter, BS), f32),
    )

    def prepare(t, place, own, own_core, other, other_core):
        return call(
            functools.partial(prepare_kernel, quarter, place),
            ready_shapes,
            [pltpu.VMEM((4 * quarter, BS), f32)],
            K["prep"][t - 1],
        )(in_specs=[SMEM] + [VMEM] * (3 + len(other_core)))(ids, own, own_core, other, *other_core)

    diag_first = diag_inverse[0]
    keep, send = call(
        functools.partial(first_kernel, quarter),
        (piece, shape((blocks * quarter + 8, BS), f32)),
        [pltpu.VMEM((4 * quarter, BS), f32), pltpu.VMEM((blocks, 2 * quarter, BS), f32)],
        K["first"],
    )(in_specs=[SMEM, SMEM, VMEM, VMEM, VMEM, VMEM])(
        ids, block_lists, diag_first, to_core(diag_inverse), right_sides, to_core(right_sides)
    )
    got = to_row(send, 1)

    groups = K["groups"]
    rest = []
    for g, group in enumerate(groups):
        diag, below, sides, _ = lax.optimization_barrier(
            (diag_inverse, factor_below, right_sides, {"first": diag_first, "send": send}[K["rest"][g]])
        )
        rows = [jnp.concatenate([diag[t], below[t - 1], sides[t]], axis=1) for t in group]
        rest.append(jnp.concatenate(rows, axis=0))
    rest_core = [to_core(a) for a in rest]

    share = keep + got[: blocks * quarter].reshape(blocks, quarter, BS)
    told = got[blocks * quarter, : (S - 1) * listed].reshape(S - 1, listed).astype(jnp.int32)

    gates = {"none": None, "send": send, "share0": share, "core1": rest_core[0]}
    stored, first = (), K["early"]
    others, other_cores = {}, {}

    def bulk():
        for u, name in enumerate(K["bulk"][: len(groups)]):
            if u not in others and name in gates:
                g = gates[name]
                others[u] = to_row(after(rest[u], g) if g is not None else rest[u], 1)

    for t in range(1, S):
        bulk()
        keep, recv = total(share)
        gates[f"recv{t - 1}"] = recv
        bulk()
        u = [t in group for group in groups].index(True)
        if u not in other_cores:
            g = K["swap"][u]
            gated = after(others[u], gates[g]) if g else others[u]
            rows = gated.shape[0] // K["cut"][u]
            other_cores[u] = [to_core(gated[i : i + rows]) for i in range(0, gated.shape[0], rows)]
        gates[f"other{t}"] = other_cores[u][-1]
        bulk()
        if t == 1 and top == 2:
            pieces = other_cores[u]
            operands = (rest[u], rest_core[u], others[u], *pieces, keep, recv)
            kernel = functools.partial(whole_step_kernel, quarter, groups[u].index(t), t, len(pieces))
            solved, share = call(
                kernel,
                (shape((blocks, quarter, BS), f32), piece),
                [pltpu.VMEM(a.shape, a.dtype) for a in ready_shapes] + [pltpu.VMEM((4 * quarter, BS), f32)],
                K["step"][0],
            )(in_specs=[SMEM] * 3 + [VMEM] * len(operands))(ids, block_lists, told, *operands)
            stored = (solved,)
            gates["share1"] = share
            continue
        ready = prepare(t, groups[u].index(t), rest[u], rest_core[u], others[u], other_cores[u])
        operands = (*stored, keep, recv, *ready)
        gates[f"prep{t}"] = operands[-1]
        bulk()
        solved_shape = shape((t * blocks, quarter, BS), f32)
        if t < S - 1 or top > 2:
            solved, share = call(
                functools.partial(step_kernel, t), (solved_shape, piece), (), K["step"][t - 1]
            )(in_specs=[SMEM, SMEM] + [VMEM] * len(operands))(block_lists, told, *operands)
            stored = (solved,)
            gates[f"share{t}"] = share
            if t == S - 2 and first:
                early = shape((first, quarter, BS), f32)
                early_kept, near = call(early_kernel, (early, early))(in_specs=[SMEM, VMEM])(ids, solved)
                near = to_row(near, 1)
                placed = [early_kept, near, to_core(early_kept), to_core(near)]

    block = shape((quarter, BS), f32)
    kept = shape((S - first, quarter, BS), f32)
    gifts = (kept, kept, block, block)
    if top > 2:
        bit = 2
        while bit < top:
            share = share + to_row(share, bit)
            bit *= 2
        own, *sent = call(functools.partial(give, first), gifts)(in_specs=[SMEM, VMEM, VMEM])(ids, solved, share)
    else:
        own, *sent = call(
            functools.partial(last_kernel, first),
            gifts,
            [pltpu.VMEM(solved_shape.shape, f32), pltpu.VMEM(piece.shape, f32)],
            K["step"][S - 2],
        )(in_specs=[SMEM] * 3 + [VMEM] * len(operands))(ids, block_lists, told, *operands)
    near, far, both = [to_row(a, bit) for a, bit in zip(sent, (1, top, top + 1))]
    if K["meet"]:
        near, far, both = lax.optimization_barrier((near, far, both))
    quarters = [own, far, near, both]
    quarters += [to_core(a) for a in quarters]
    if first:
        quarters += placed
    return call(
        functools.partial(place_kernel, quarter, first),
        shape((S, BS // 2, 4 * quarter), f32),
        [pltpu.VMEM((S, 4 * quarter, BS), f32)],
    )(in_specs=[SMEM] + [VMEM] * len(quarters))(ids, *quarters)


def solution(mesh):
    in_specs = (
        P("grp", ("row", "sub"), "rhs"),
        P("grp", ("row", "sub"), None),
        P("grp", ("row", "sub"), None),
        P("grp", "row", None),
    )
    out_specs = P("grp", ("row", "sub"), "rhs")
    step = functools.partial(body, mesh.shape["row"])
    return jax.shard_map(step, mesh=mesh, in_specs=in_specs, out_specs=out_specs, check_vma=False)
```
